32 devices in a mesh: dp: 2 (over y), expert: 16 (over z, x, core).
Axes of the slice: x: 2, y: 2, z: 4, core: 2. Of those that a mesh axis runs over, the one named last changes fastest.
Arguments:
- tokens: bfloat16 [8192, 1024], P(('dp', 'expert')), may hold values from -6 to 6
- cotangent: bfloat16 [8192, 1024], P(('dp', 'expert')), may hold values from -1.1953125 to 1.1953125
- prob: bfloat16 [8192], P(('dp', 'expert')), may hold values from 0.19921875 to 1
- assign: int32 [8192, 1], P(('dp', 'expert')), may hold values from 0 to 15; in each aligned block of 256 rows (0 to 255, 256 to 511, ...) at most 48 rows name the same one
- w_gate: bfloat16 [16, 1024, 1024], P('expert'), may hold values from -0.1875 to 0.1875
- w_up: bfloat16 [16, 1024, 1024], P('expert'), may hold values from -0.1875 to 0.1875
- w_down: bfloat16 [16, 1024, 1024], P('expert'), may hold values from -0.1875 to 0.1875
Outputs:
- grad_tokens: bfloat16 [8192, 1024], P(('dp', 'expert'))
- grad_prob: bfloat16 [8192], P(('dp', 'expert'))
- grad_gate: float32 [16, 1024, 1024], P('expert', 'dp')
- grad_up: float32 [16, 1024, 1024], P('expert', 'dp')
- grad_down: float32 [16, 1024, 1024], P('expert', 'dp')
The draws below stay inside these ranges and needn't reach their ends.
Inputs may be any that keep to these rules, and one draw needn't show every extreme that they name: `assign`: among the 256 tokens of one device (aligned blocks of rows), at most 48 are assigned to one expert, and in every draw some expert receives exactly 48 tokens of some device.
All inputs are finite; a program needn't handle non-finite values.
Results may differ from the reference program's by a relative error of at most 0.015.
Values may be sent and summed in bfloat16 or wider, within the bound.
A program may use at most 128 MiB of HBM per device.

```python
import math
import jax
import jax.numpy as jnp
import numpy as np
from jax import lax

D = 1024
FF = 1024
TOK_DEV = 256
EXPERTS = 16
GROUPS = 2
MOST = 48
TOKENS = 8192


def block_scale(rng, dims, cuts, smallest, top_value):
    def one(dim, parts):
        heights = jax.random.uniform(jax.random.fold_in(jax.random.fold_in(rng, 6), dim), (parts,), jnp.float32, smallest / len(cuts), top_value / len(cuts))
        return jnp.repeat(jnp.exp(heights), dims[dim] // parts).reshape((-1,) + (1,) * (len(dims) - dim - 1))

    level = one(*cuts[0])
    for cut in cuts[1:]:
        level = level * one(*cut)
    return level


def assign_block(stream_key, own, number, rows, number_of, top, limit, skew):
    sequence = jax.random.permutation(stream_key, number_of)
    heavy_load, ordinary = portions_of(number_of, rows * top, limit, skew, True), portions_of(number_of, rows * top, limit, skew, False)
    places = jnp.arange(number_of)

    def named(sizes, turn):
        used = int((sizes > 0).sum())
        fixed = max(1, used // 4)
        passed = fixed + (places - fixed + turn * (used - fixed)) % max(1, number_of - fixed)
        return jnp.zeros((number_of,), jnp.int32).at[sequence[jnp.where(places < fixed, places, passed)]].set(jnp.asarray(sizes, jnp.int32))

    sizes = jnp.where(number % 4 == 0, named(heavy_load, number // 4), named(ordinary, number - number // 4 - 1))
    mixed = jax.random.permutation(jax.random.fold_in(own, 3), number_of)
    giver, sink = mixed[0:number_of // 2 * 2:2], mixed[1:number_of // 2 * 2:2]
    room = jnp.minimum(sizes[giver] - 1, limit - sizes[sink]) // 2
    room = jnp.where((giver == sequence[0]) | (sink == sequence[0]) | (sizes[sink] == 0), 0, jnp.maximum(room, 0))
    passed = jax.random.randint(jax.random.fold_in(own, 4), (number_of // 2,), 0, 1 << 20) % (room + 1)
    sizes = sizes.at[giver].add(-passed).at[sink].add(passed)
    labels = jnp.searchsorted(jnp.cumsum(sizes), jnp.arange(rows * top), side="right").astype(jnp.int32)
    grid = labels.reshape(top, rows).T
    grid = grid[jax.random.permutation(jax.random.fold_in(own, 1), rows)]
    turn = jax.random.randint(jax.random.fold_in(own, 2), (rows, 1), 0, top)
    return jnp.take_along_axis(grid, (jnp.arange(top)[None, :] + turn) % top, axis=1)


def portions_of(number_of, total, limit, slope, full):
    loads = [(1 << 20) // math.isqrt(rank ** slope) + 1 for rank in range(1, number_of + 1)]
    largest = limit if full else min(limit, max(-(-total // number_of), total * loads[0] // sum(loads)))
    least = 1 if total - largest >= number_of - 1 else 0
    given, spare = [largest] + [least] * (number_of - 1), total - largest - least * (number_of - 1)
    while spare > 0:
        candidates = [i for i in range(1, number_of) if given[i] < largest] or [i for i in range(1, number_of) if given[i] < limit]
        mass, remaining = sum([loads[i] for i in candidates]), spare
        for i in candidates:
            extra = min(limit - given[i], max(1, remaining * loads[i] // mass), spare)
            given[i] = given[i] + extra
            spare = spare - extra
    return np.array(given)


def bell_draw(own_key, extent, spread, bound, split=(), held_as=jnp.bfloat16):
    values = spread * jax.random.normal(own_key, extent, jnp.float32)
    if split:
        values = values * block_scale(own_key, extent, split, -0.22, 0.18)
    return jnp.clip(values, -bound, bound).astype(held_as)


def setup_inputs(seed: int = 0) -> dict:
    streams_of = jax.random.split(jax.random.key(seed), 8)
    tokens = bell_draw(streams_of[0], (TOKENS, D), 1.0, 6.0, ((0, 32),))
    cotangent = bell_draw(streams_of[1], (TOKENS, D), 0.2, 1.1953125, ((0, 32),))
    prob = jnp.clip(0.19921875 + 0.80078125 * jax.random.uniform(streams_of[2], (TOKENS,), jnp.float32) ** block_scale(streams_of[2], (TOKENS,), ((0, 32),), -0.2, 0.2), 0.19921875, 1.0).astype(jnp.bfloat16)
    assign_keys = jax.random.split(jax.random.fold_in(streams_of[3], 1), TOKENS // TOK_DEV)
    assign_turns = jax.random.permutation(jax.random.fold_in(streams_of[3], 3), TOKENS // TOK_DEV)
    assign = jax.vmap(lambda own, number: assign_block(jax.random.fold_in(streams_of[3], 2), own, number, TOK_DEV, EXPERTS, 1, MOST, 2))(assign_keys, assign_turns).reshape((TOKENS, 1))
    w_gate = bell_draw(streams_of[4], (EXPERTS, D, FF), D ** -0.5, 0.1875, ((0, 16),))
    w_up = bell_draw(streams_of[5], (EXPERTS, D, FF), D ** -0.5, 0.1875, ((0, 16),))
    w_down = bell_draw(streams_of[6], (EXPERTS, FF, D), FF ** -0.5, 0.1875, ((0, 16),))
    return {"tokens": tokens, "cotangent": cotangent, "prob": prob, "assign": assign, "w_gate": w_gate, "w_up": w_up, "w_down": w_down}


def placement_of(assign_dev):
    chosen = (assign_dev[:, None] == jnp.arange(EXPERTS, dtype=jnp.int32)[None, :]).astype(jnp.int32)
    before = jnp.cumsum(chosen, axis=0) - chosen
    position = jnp.sum(before * chosen, axis=1).astype(jnp.int32)
    slot = assign_dev * MOST + position
    return jnp.arange(EXPERTS * MOST, dtype=jnp.int32)[:, None] == slot[None, :]


def expert_pass(rows_in, cot_in, prob_in, gate_weight, up_weight, down_weight):
    gate = jnp.dot(rows_in, gate_weight, preferred_element_type=jnp.float32)
    up = jnp.dot(rows_in, up_weight, preferred_element_type=jnp.float32)
    sigmoid_gate = jax.nn.sigmoid(gate)
    activation = gate * sigmoid_gate
    hidden = (activation * up).astype(jnp.bfloat16)
    expert_out = jnp.dot(hidden, down_weight, preferred_element_type=jnp.float32)
    grad_prob = jnp.sum(cot_in.astype(jnp.float32) * expert_out, axis=1).astype(jnp.bfloat16)
    scaled = (prob_in.astype(jnp.float32)[:, None] * cot_in.astype(jnp.float32)).astype(jnp.bfloat16)
    grad_hidden = lax.dot_general(scaled, down_weight, (((1,), (1,)), ((), ())), preferred_element_type=jnp.float32)
    grad_gate_pre = (grad_hidden * up * sigmoid_gate * (1.0 + gate * (1.0 - sigmoid_gate))).astype(jnp.bfloat16)
    grad_up_pre = (grad_hidden * activation).astype(jnp.bfloat16)
    grad_rows = lax.dot_general(grad_gate_pre, gate_weight, (((1,), (1,)), ((), ())), preferred_element_type=jnp.float32)
    grad_rows = grad_rows + lax.dot_general(grad_up_pre, up_weight, (((1,), (1,)), ((), ())), preferred_element_type=jnp.float32)
    grad_rows = grad_rows.astype(jnp.bfloat16)
    part_gate = lax.dot_general(rows_in, grad_gate_pre, (((0,), (0,)), ((), ())), preferred_element_type=jnp.float32)
    part_up = lax.dot_general(rows_in, grad_up_pre, (((0,), (0,)), ((), ())), preferred_element_type=jnp.float32)
    part_down = lax.dot_general(hidden, scaled, (((0,), (0,)), ((), ())), preferred_element_type=jnp.float32)
    return grad_rows, grad_prob, part_gate, part_up, part_down


def rounded(value):
    return lax.optimization_barrier(value.astype(jnp.bfloat16)).astype(jnp.float32)


def reference(tokens, cotangent, prob, assign, w_gate, w_up, w_down):
    devices = GROUPS * EXPERTS
    slots_all = EXPERTS * MOST
    tok_split = tokens.reshape(devices, TOK_DEV, D)
    cot_split = cotangent.reshape(devices, TOK_DEV, D)
    prob_split = prob.reshape(devices, TOK_DEV)
    assign_split = assign.reshape(devices, TOK_DEV).astype(jnp.int32)

    def gather_slots(item):
        tok_dev, cot_dev, prob_dev, assign_dev = item
        place = placement_of(assign_dev)
        weights = place.astype(jnp.bfloat16)
        send_rows = jnp.dot(weights, tok_dev, preferred_element_type=jnp.float32).astype(jnp.bfloat16)
        send_cot = jnp.dot(weights, cot_dev, preferred_element_type=jnp.float32).astype(jnp.bfloat16)
        send_prob = jnp.sum(jnp.where(place, prob_dev[None, :].astype(jnp.float32), 0.0), axis=1).astype(jnp.bfloat16)
        return send_rows, send_cot, send_prob

    send_rows, send_cot, send_prob = lax.map(gather_slots, (tok_split, cot_split, prob_split, assign_split))
    rows_by_expert = send_rows.reshape(GROUPS, EXPERTS, EXPERTS, MOST, D).transpose(2, 0, 1, 3, 4).reshape(EXPERTS, GROUPS, slots_all, D)
    cot_by_expert = send_cot.reshape(GROUPS, EXPERTS, EXPERTS, MOST, D).transpose(2, 0, 1, 3, 4).reshape(EXPERTS, GROUPS, slots_all, D)
    prob_by_expert = send_prob.reshape(GROUPS, EXPERTS, EXPERTS, MOST).transpose(2, 0, 1, 3).reshape(EXPERTS, GROUPS, slots_all)

    def per_expert(item):
        rows_e, cot_e, prob_e, gate_weight, up_weight, down_weight = item

        def per_group(carry, inner):
            rows_in, cot_in, prob_in = inner
            grad_rows, grad_pr, part_gate, part_up, part_down = expert_pass(rows_in, cot_in, prob_in, gate_weight, up_weight, down_weight)
            carry = (carry[0] + rounded(part_gate), carry[1] + rounded(part_up), carry[2] + rounded(part_down))
            return carry, (grad_rows, grad_pr)

        start = (jnp.zeros((D, FF), jnp.float32), jnp.zeros((D, FF), jnp.float32), jnp.zeros((FF, D), jnp.float32))
        carry, (grad_rows, grad_pr) = lax.scan(per_group, start, (rows_e, cot_e, prob_e))
        return grad_rows, grad_pr, carry[0], carry[1], carry[2]

    grad_rows, grad_pr, grad_gate, grad_up, grad_down = lax.map(per_expert, (rows_by_expert, cot_by_expert, prob_by_expert, w_gate, w_up, w_down))
    back_rows = grad_rows.reshape(EXPERTS, GROUPS, EXPERTS, MOST, D).transpose(1, 2, 0, 3, 4).reshape(devices, slots_all, D)
    back_prob = grad_pr.reshape(EXPERTS, GROUPS, EXPERTS, MOST).transpose(1, 2, 0, 3).reshape(devices, slots_all)

    def scatter_back(item):
        rows_back, prob_back, assign_dev = item
        place = placement_of(assign_dev)
        weights = place.astype(jnp.bfloat16)
        grad_tok = lax.dot_general(weights, rows_back, (((0,), (0,)), ((), ())), preferred_element_type=jnp.float32).astype(jnp.bfloat16)
        grad_p = jnp.sum(jnp.where(place, prob_back[:, None].astype(jnp.float32), 0.0), axis=0).astype(jnp.bfloat16)
        return grad_tok, grad_p

    grad_tokens, grad_prob = lax.map(scatter_back, (back_rows, back_prob, assign_split))
    return grad_tokens.reshape(TOKENS, D), grad_prob.reshape(TOKENS), grad_gate, grad_up, grad_down
```

```python
import functools
import math

import jax
import jax.numpy as jnp
from jax import lax
from jax.experimental import pallas as pl
from jax.experimental.pallas import tpu as pltpu
from jax.sharding import PartitionSpec as P

MESH = pl.DeviceIdType.MESH
F32 = jnp.float32
BF16 = jnp.bfloat16
BLOCK_ORDER = (2, 3, 1, 0)
BLOCKS = 4


def tn(a, b):
    return lax.dot_general(a, b, (((0,), (0,)), ((), ())), preferred_element_type=F32)


def nt(a, b):
    return lax.dot_general(a, b, (((1,), (1,)), ((), ())), preferred_element_type=F32)


def nn(a, b):
    return jnp.dot(a, b, preferred_element_type=F32)


def kernel(
    n, ndp, cap,
    tok, cot, prob, assign, wg_hbm, wu_hbm, wd_hbm,
    gt_out, gp_out, gg_out, gu_out, gd_out,
    wg, wu, wd, st, ss, rt, rs, hid, ggp, gup, acc, bs, br, ps, pr,
    w_sem, st_s, st_r, ss_s, ss_r, ft_s, ft_r, fs_s, fs_r, b_s, b_r, p_s, p_r, o_sem,
):
    k = lax.axis_index("dp")
    me = lax.axis_index("expert")
    own_tokens, width = tok.shape
    ff = wg.shape[1]
    per = n // BLOCKS
    rows = per * cap
    half = acc.shape[1]
    my_block, my_place = me // per, lax.rem(me, per)

    def block_of(c):
        high = lax.rem(my_block // 2 + c // 2, 2)
        low = lax.rem(lax.rem(my_block, 2) + c % 2, 2)
        return high * 2 + low

    def partner(c, j):
        return block_of(c) * per + lax.rem(my_place + j, per)

    def slot_rows(s):
        return pl.ds(pl.multiple_of(s * cap, 16), cap)

    def block_rows(b):
        return pl.ds(pl.multiple_of(b * rows, 16), rows)

    barrier = pltpu.get_barrier_semaphore()
    for c in range(BLOCKS):
        for j in range(per):
            if c or j:
                pl.semaphore_signal(
                    barrier, inc=1, device_id=(k, partner(c, j)), device_id_type=MESH
                )
    for j in range(1, ndp):
        pl.semaphore_signal(
            barrier, inc=1, device_id=(lax.rem(k + j, ndp), me), device_id_type=MESH
        )

    weights = [
        pltpu.make_async_copy(src, dst, w_sem.at[i])
        for i, (src, dst) in enumerate(((wg_hbm, wg), (wu_hbm, wu), (wd_hbm, wd)))
    ]
    for copy in weights:
        copy.start()

    expert = lax.broadcasted_iota(jnp.int32, (n, own_tokens), 0)
    chosen = (expert == assign[...]).astype(F32)
    earlier = (
        lax.broadcasted_iota(jnp.int32, (own_tokens, own_tokens), 0)
        < lax.broadcasted_iota(jnp.int32, (own_tokens, own_tokens), 1)
    ).astype(F32)
    before = nn(chosen.astype(BF16), earlier.astype(BF16))
    slot = jnp.sum(chosen * (before + expert.astype(F32) * cap), axis=0, keepdims=True)
    slot = slot.astype(jnp.int32)
    prob_row = prob[...].astype(F32)

    def place(b):
        return lax.broadcasted_iota(jnp.int32, (rows, own_tokens), 0) + b * rows == slot

    def to_slot(src, dst, s, send, recv, c, j):
        return pltpu.make_async_remote_copy(
            src_ref=src,
            dst_ref=dst,
            send_sem=send.at[c * per + j],
            recv_sem=recv.at[me],
            device_id=(k, s),
            device_id_type=MESH,
        )

    def out_tok(c, j):
        s = partner(c, j)
        return to_slot(st.at[slot_rows(s)], rt.at[k, slot_rows(me)], s, st_s, st_r, c, j)

    def out_cot(c, j):
        s = partner(c, j)
        return to_slot(ss.at[slot_rows(s)], rs.at[k, slot_rows(me)], s, ss_s, ss_r, c, j)

    def back_grad(c, j):
        s = partner(c, j)
        return to_slot(bs.at[slot_rows(s)], br.at[slot_rows(me)], s, b_s, b_r, c, j)

    def back_prob(c, j):
        s = partner(c, j)
        return to_slot(ps.at[s], pr.at[me], s, p_s, p_r, c, j)

    def arrived(buf, s, recv):
        pltpu.make_async_remote_copy(
            src_ref=buf, dst_ref=buf, send_sem=st_s.at[0], recv_sem=recv.at[s],
            device_id=(k, s), device_id_type=MESH,
        ).wait_recv()

    for step, c in enumerate(BLOCK_ORDER):
        b = block_of(c)
        here = place(b)
        st[block_rows(b), :] = nn(here.astype(F32).astype(BF16), tok[...]).astype(BF16)
        if step == 0:
            pl.semaphore_wait(barrier, n - 1 + ndp - 1)
        for j in range(per):
            if c or j:
                out_tok(c, j).start()
        ss[block_rows(b), :] = nn(
            jnp.where(here, prob_row, 0.0).astype(BF16), cot[...]
        ).astype(BF16)
        for j in range(per):
            if c or j:
                out_cot(c, j).start()
    rt[k, slot_rows(me), :] = st[slot_rows(me), :]
    rs[k, slot_rows(me), :] = ss[slot_rows(me), :]

    def forward(buf, b, j, send, recv):
        view = buf.at[k, block_rows(b)]
        return pltpu.make_async_remote_copy(
            src_ref=view,
            dst_ref=view,
            send_sem=send.at[(j - 1) * BLOCKS + b],
            recv_sem=recv.at[k * BLOCKS + b],
            device_id=(lax.rem(k + j, ndp), me),
            device_id_type=MESH,
        )

    tile = min(512, ff)

    def hidden_grads(g, b):
        here = block_rows(b)

        def body(i, total):
            cols = pl.ds(pl.multiple_of(i * tile, tile), tile)
            x = rt[g, here, :]
            gate = nn(x, wg[:, cols])
            up = nn(x, wu[:, cols])
            grad = nt(rs[g, here, :], wd[cols, :])
            s = jax.nn.sigmoid(gate)
            act = gate * s
            h = (act * up).astype(BF16)
            hid[here, cols] = h
            ggp[here, cols] = (grad * up * s * (1.0 + gate * (1.0 - s))).astype(BF16)
            gup[here, cols] = (grad * act).astype(BF16)
            return total + jnp.sum(grad * h.astype(F32), axis=1, keepdims=True)

        return lax.fori_loop(0, ff // tile, body, jnp.zeros((rows, 1), F32))

    diagonal = lax.broadcasted_iota(jnp.int32, (per, cap, 128), 1) == lax.broadcasted_iota(
        jnp.int32, (per, cap, 128), 2
    )

    def own_block(c):
        b = block_of(c)
        here = block_rows(b)
        dots = hidden_grads(k, b)

        def body(i, carry):
            cols = pl.ds(pl.multiple_of(i * tile, tile), tile)
            grad = nt(ggp[here, :], wg[cols, :]) + nt(gup[here, :], wu[cols, :])
            bs[here, cols] = grad.astype(BF16)
            return carry

        lax.fori_loop(0, width // tile, body, 0)
        line = jnp.sum(jnp.where(diagonal, dots.reshape(per, cap, 1), 0.0), axis=1, keepdims=True)
        ps[pl.ds(b * per, per)] = jnp.broadcast_to(line, (per, 8, 128))
        for j in range(per):
            if c or j:
                back_grad(c, j).start()
                back_prob(c, j).start()
        if c == 0:
            br[slot_rows(me), :] = bs[slot_rows(me), :]
            pr[me] = ps[me]

    for c in BLOCK_ORDER:
        b = block_of(c)
        for j in range(per):
            if c or j:
                s = partner(c, j)
                arrived(rt.at[k, slot_rows(s)], s, st_r)
        for j in range(1, ndp):
            forward(rt, b, j, ft_s, ft_r).start()
        for j in range(per):
            if c or j:
                s = partner(c, j)
                arrived(rs.at[k, slot_rows(s)], s, ss_r)
        for j in range(1, ndp):
            forward(rs, b, j, fs_s, fs_r).start()
        if c == BLOCK_ORDER[0]:
            for copy in weights:
                copy.wait()
        own_block(c)

    mt = math.gcd(256, half)

    def weight_grads(g, first):
        def body(i, carry):
            out = pl.ds(pl.multiple_of(i * mt, mt), mt)
            src = pl.ds(pl.multiple_of(k * half + i * mt, mt), mt)
            x = rt[g, :, src]
            terms = (tn(x, ggp[...]), tn(x, gup[...]), tn(hid[:, src], rs[g]))
            for m in range(3):
                if first:
                    acc[m, out, :] = terms[m]
                else:
                    acc[m, out, :] += terms[m]
            return carry

        lax.fori_loop(0, half // mt, body, 0)

    weight_grads(k, True)

    def peer(j, carry):
        g = lax.rem(k + j, ndp)
        for c in BLOCK_ORDER:
            b = block_of(c)
            for buf, recv in ((rt, ft_r), (rs, fs_r)):
                view = buf.at[g, block_rows(b)]
                pltpu.make_async_remote_copy(
                    src_ref=view, dst_ref=view, send_sem=ft_s.at[0],
                    recv_sem=recv.at[g * BLOCKS + b],
                    device_id=(g, me), device_id_type=MESH,
                ).wait_recv()
            hidden_grads(g, b)
        weight_grads(g, False)
        return carry

    lax.fori_loop(1, ndp, peer, 0)
    outs = [
        pltpu.make_async_copy(acc.at[m], dst, o_sem.at[m])
        for m, dst in enumerate((gg_out, gu_out, gd_out))
    ]
    for copy in outs:
        copy.start()

    total = jnp.zeros((1, own_tokens), F32)
    grads = jnp.zeros((own_tokens, width), F32)
    for c in reversed(BLOCK_ORDER):
        b = block_of(c)
        for j in range(per):
            if c or j:
                s = partner(c, j)
                arrived(br.at[slot_rows(s)], s, b_r)
                arrived(pr.at[s], s, p_r)
        here = place(b).astype(F32)
        grads = grads + tn(here.astype(BF16), br[block_rows(b), :])
        line = pr[pl.ds(b * per, per)][:, 0:1, :]
        column = jnp.sum(jnp.where(diagonal, line, 0.0), axis=2, keepdims=True)
        total = total + jnp.sum(here * column.reshape(rows, 1), axis=0, keepdims=True)
    gt_out[...] = grads.astype(BF16)
    gp_out[...] = (total / prob_row).astype(BF16)

    for c in BLOCK_ORDER:
        for j in range(per):
            if c or j:
                for make in (out_tok, out_cot, back_grad, back_prob):
                    make(c, j).wait_send()
        for j in range(1, ndp):
            forward(rt, block_of(c), j, ft_s, ft_r).wait_send()
            forward(rs, block_of(c), j, fs_s, fs_r).wait_send()
    for copy in outs:
        copy.wait()


def local(n, ndp, tokens, cotangent, prob, assign, w_gate, w_up, w_down):
    own_tokens, width = tokens.shape
    ff = w_gate.shape[2]
    cap = -(-(3 * own_tokens // n) // 16) * 16
    slots = n * cap
    vmem, anywhere = pl.BlockSpec(memory_space=pltpu.VMEM), pl.BlockSpec(memory_space=pl.ANY)
    dma = pltpu.SemaphoreType.DMA
    shape = jax.ShapeDtypeStruct
    grad_tokens, grad_prob, grad_gate, grad_up, grad_down = pl.pallas_call(
        functools.partial(kernel, n, ndp, cap),
        out_shape=(
            shape((own_tokens, width), BF16),
            shape((1, own_tokens), BF16),
            shape((width // ndp, ff), F32),
            shape((width // ndp, ff), F32),
            shape((ff // ndp, width), F32),
        ),
        in_specs=[vmem] * 4 + [anywhere] * 3,
        out_specs=(vmem, vmem, anywhere, anywhere, anywhere),
        scratch_shapes=[
            pltpu.VMEM((width, ff), BF16),
            pltpu.VMEM((width, ff), BF16),
            pltpu.VMEM((ff, width), BF16),
            pltpu.VMEM((slots, width), BF16),
            pltpu.VMEM((slots, width), BF16),
            pltpu.VMEM((ndp, slots, width), BF16),
            pltpu.VMEM((ndp, slots, width), BF16),
            pltpu.VMEM((slots, ff), BF16),
            pltpu.VMEM((slots, ff), BF16),
            pltpu.VMEM((slots, ff), BF16),
            pltpu.VMEM((3, width // ndp, ff), F32),
            pltpu.VMEM((slots, width), BF16),
            pltpu.VMEM((slots, width), BF16),
            pltpu.VMEM((n, 8, 128), F32),
            pltpu.VMEM((n, 8, 128), F32),
            dma((3,)),
            dma((n,)), dma((n,)), dma((n,)), dma((n,)),
            dma((ndp * BLOCKS,)), dma((ndp * BLOCKS,)),
            dma((ndp * BLOCKS,)), dma((ndp * BLOCKS,)),
            dma((n,)), dma((n,)), dma((n,)), dma((n,)),
            dma((3,)),
        ],
        compiler_params=pltpu.CompilerParams(
            collective_id=0, has_side_effects=True, vmem_limit_bytes=62 * 2**20
        ),
        cost_estimate=pl.CostEstimate(
            flops=22 * slots * width * ff, bytes_accessed=16 * width * ff, transcendentals=0
        ),
    )(
        tokens, cotangent, prob.reshape(1, own_tokens), assign.reshape(1, own_tokens),
        w_gate[0], w_up[0], w_down[0],
    )
    return (
        grad_tokens, grad_prob.reshape(own_tokens),
        grad_gate[None], grad_up[None], grad_down[None],
    )


def solution(mesh):
    placed = (
        P(("dp", "expert"), None),
        P(("dp", "expert"), None),
        P(("dp", "expert")),
        P(("dp", "expert"), None),
        P("expert", None, None),
        P("expert", None, None),
        P("expert", None, None),
    )
    return jax.shard_map(
        functools.partial(local, mesh.shape["expert"], mesh.shape["dp"]),
        mesh=mesh,
        in_specs=placed,
        out_specs=(
            P(("dp", "expert"), None),
            P(("dp", "expert")),
            P("expert", "dp", None),
            P("expert", "dp", None),
            P("expert", "dp", None),
        ),
        check_vma=False,
    )
```

```python
import functools
import math

import jax
import jax.numpy as jnp
from jax import lax
from jax.experimental import pallas as pl
from jax.experimental.pallas import tpu as pltpu
from jax.sharding import PartitionSpec as P

MESH = pl.DeviceIdType.MESH
F32 = jnp.float32
BF16 = jnp.bfloat16
BLOCK_ORDER = (0, 2, 1, 3)
BLOCKS = 4


def tn(a, b):
    return lax.dot_general(a, b, (((0,), (0,)), ((), ())), preferred_element_type=F32)


def nt(a, b):
    return lax.dot_general(a, b, (((1,), (1,)), ((), ())), preferred_element_type=F32)


def nn(a, b):
    return jnp.dot(a, b, preferred_element_type=F32)


def kernel(
    n, ndp, cap,
    tok, cot, prob, assign, wg_hbm, wu_hbm, wd_hbm,
    gt_out, gp_out, gg_out, gu_out, gd_out,
    wg, wu, wd, st, ss, rt, rs, hid, ggp, gup, acc, bs, br, ps, pr,
    w_sem, st_s, st_r, ss_s, ss_r, ft_s, ft_r, fs_s, fs_r, b_s, b_r, p_s, p_r, o_sem,
):
    k = lax.axis_index("dp")
    me = lax.axis_index("expert")
    own_tokens, width = tok.shape
    ff = wg.shape[1]
    per = n // BLOCKS
    rows = per * cap
    half = acc.shape[1]
    my_block, my_place = me // per, lax.rem(me, per)

    def block_of(c):
        high = lax.rem(my_block // 2 + c // 2, 2)
        low = lax.rem(lax.rem(my_block, 2) + c % 2, 2)
        return high * 2 + low

    def partner(c, j):
        return block_of(c) * per + lax.rem(my_place + j, per)

    def slot_rows(s):
        return pl.ds(pl.multiple_of(s * cap, 16), cap)

    def block_rows(b):
        return pl.ds(pl.multiple_of(b * rows, 16), rows)

    barrier = pltpu.get_barrier_semaphore()
    for c in range(BLOCKS):
        for j in range(per):
            if c or j:
                pl.semaphore_signal(
                    barrier, inc=1, device_id=(k, partner(c, j)), device_id_type=MESH
                )
    for j in range(1, ndp):
        pl.semaphore_signal(
            barrier, inc=1, device_id=(lax.rem(k + j, ndp), me), device_id_type=MESH
        )

    weights = [
        pltpu.make_async_copy(src, dst, w_sem.at[i])
        for i, (src, dst) in enumerate(((wg_hbm, wg), (wu_hbm, wu), (wd_hbm, wd)))
    ]
    for copy in weights:
        copy.start()

    expert = lax.broadcasted_iota(jnp.int32, (n, own_tokens), 0)
    chosen = (expert == assign[...]).astype(F32)
    earlier = (
        lax.broadcasted_iota(jnp.int32, (own_tokens, own_tokens), 0)
        < lax.broadcasted_iota(jnp.int32, (own_tokens, own_tokens), 1)
    ).astype(F32)
    before = nn(chosen.astype(BF16), earlier.astype(BF16))
    slot = jnp.sum(chosen * (before + expert.astype(F32) * cap), axis=0, keepdims=True)
    slot = slot.astype(jnp.int32)
    prob_row = prob[...].astype(F32).reshape(1, own_tokens)

    def place(b):
        return lax.broadcasted_iota(jnp.int32, (rows, own_tokens), 0) + b * rows == slot

    def to_slot(src, dst, s, send, recv, c, j):
        return pltpu.make_async_remote_copy(
            src_ref=src,
            dst_ref=dst,
            send_sem=send.at[c * per + j],
            recv_sem=recv.at[me],
            device_id=(k, s),
            device_id_type=MESH,
        )

    def out_tok(c, j):
        s = partner(c, j)
        return to_slot(st.at[slot_rows(s)], rt.at[k, slot_rows(me)], s, st_s, st_r, c, j)

    def out_cot(c, j):
        s = partner(c, j)
        return to_slot(ss.at[slot_rows(s)], rs.at[k, slot_rows(me)], s, ss_s, ss_r, c, j)

    def back_grad(c, j):
        s = partner(c, j)
        return to_slot(bs.at[slot_rows(s)], br.at[slot_rows(me)], s, b_s, b_r, c, j)

    def back_prob(c, j):
        s = partner(c, j)
        return to_slot(ps.at[s], pr.at[me], s, p_s, p_r, c, j)

    def arrived(buf, s, recv):
        pltpu.make_async_remote_copy(
            src_ref=buf, dst_ref=buf, send_sem=st_s.at[0], recv_sem=recv.at[s],
            device_id=(k, s), device_id_type=MESH,
        ).wait_recv()

    for step, c in enumerate(BLOCK_ORDER):
        b = block_of(c)
        here = place(b)
        st[block_rows(b), :] = nn(here.astype(F32).astype(BF16), tok[...]).astype(BF16)
        if step == 0:
            pl.semaphore_wait(barrier, n - 1 + ndp - 1)
        for j in range(per):
            if c or j:
                out_tok(c, j).start()
        ss[block_rows(b), :] = nn(
            jnp.where(here, prob_row, 0.0).astype(BF16), cot[...]
        ).astype(BF16)
        for j in range(per):
            if c or j:
                out_cot(c, j).start()
    rt[k, slot_rows(me), :] = st[slot_rows(me), :]
    rs[k, slot_rows(me), :] = ss[slot_rows(me), :]

    def forward(buf, b, j, send, recv):
        view = buf.at[k, block_rows(b)]
        return pltpu.make_async_remote_copy(
            src_ref=view,
            dst_ref=view,
            send_sem=send.at[(j - 1) * BLOCKS + b],
            recv_sem=recv.at[k * BLOCKS + b],
            device_id=(lax.rem(k + j, ndp), me),
            device_id_type=MESH,
        )

    tile = min(512, ff)

    def hidden_grads(g, b):
        here = block_rows(b)

        def body(i, total):
            cols = pl.ds(pl.multiple_of(i * tile, tile), tile)
            x = rt[g, here, :]
            gate = nn(x, wg[:, cols])
            up = nn(x, wu[:, cols])
            grad = nt(rs[g, here, :], wd[cols, :])
            s = jax.nn.sigmoid(gate)
            act = gate * s
            h = (act * up).astype(BF16)
            hid[:, cols] = h
            ggp[:, cols] = (grad * up * s * (1.0 + gate * (1.0 - s))).astype(BF16)
            gup[:, cols] = (grad * act).astype(BF16)
            return total + jnp.sum(grad * h.astype(F32), axis=1, keepdims=True)

        return lax.fori_loop(0, ff // tile, body, jnp.zeros((rows, 1), F32))

    diagonal = lax.broadcasted_iota(jnp.int32, (per, cap, 128), 1) == lax.broadcasted_iota(
        jnp.int32, (per, cap, 128), 2
    )

    def own_block(c):
        b = block_of(c)
        here = block_rows(b)
        dots = hidden_grads(k, b)

        def body(i, carry):
            cols = pl.ds(pl.multiple_of(i * tile, tile), tile)
            grad = nt(ggp[...], wg[cols, :]) + nt(gup[...], wu[cols, :])
            bs[here, cols] = grad.astype(BF16)
            return carry

        lax.fori_loop(0, width // tile, body, 0)
        line = jnp.sum(jnp.where(diagonal, dots.reshape(per, cap, 1), 0.0), axis=1, keepdims=True)
        ps[pl.ds(b * per, per)] = jnp.broadcast_to(line, (per, 8, 128))
        for j in range(per):
            if c or j:
                back_grad(c, j).start()
                back_prob(c, j).start()
        if c == 0:
            br[slot_rows(me), :] = bs[slot_rows(me), :]
            pr[me] = ps[me]

    mt = math.gcd(256, half)

    def weight_grads(g, b, first):
        here = block_rows(b)

        def body(i, carry):
            out = pl.ds(pl.multiple_of(i * mt, mt), mt)
            src = pl.ds(pl.multiple_of(k * half + i * mt, mt), mt)
            x = rt[g, here, src]
            terms = (tn(x, ggp[...]), tn(x, gup[...]), tn(hid[:, src], rs[g, here, :]))
            for m in range(3):
                if first:
                    acc[m, out, :] = terms[m]
                else:
                    acc[m, out, :] += terms[m]
            return carry

        lax.fori_loop(0, half // mt, body, 0)

    def peers_block(c):
        b = block_of(c)

        def body(j, carry):
            g = lax.rem(k + j, ndp)
            for buf, recv in ((rt, ft_r), (rs, fs_r)):
                view = buf.at[g, block_rows(b)]
                pltpu.make_async_remote_copy(
                    src_ref=view, dst_ref=view, send_sem=ft_s.at[0],
                    recv_sem=recv.at[g * BLOCKS + b],
                    device_id=(g, me), device_id_type=MESH,
                ).wait_recv()
            hidden_grads(g, b)
            weight_grads(g, b, False)
            return carry

        lax.fori_loop(1, ndp, body, 0)

    for step, c in enumerate(BLOCK_ORDER):
        b = block_of(c)
        for j in range(per):
            if c or j:
                s = partner(c, j)
                arrived(rt.at[k, slot_rows(s)], s, st_r)
        for j in range(1, ndp):
            forward(rt, b, j, ft_s, ft_r).start()
        for j in range(per):
            if c or j:
                s = partner(c, j)
                arrived(rs.at[k, slot_rows(s)], s, ss_r)
        for j in range(1, ndp):
            forward(rs, b, j, fs_s, fs_r).start()
        if step == 0:
            for copy in weights:
                copy.wait()
        own_block(c)
        weight_grads(k, b, step == 0)
        if step:
            peers_block(BLOCK_ORDER[step - 1])
    peers_block(BLOCK_ORDER[-1])
    outs = [
        pltpu.make_async_copy(acc.at[m], dst, o_sem.at[m])
        for m, dst in enumerate((gg_out, gu_out, gd_out))
    ]
    for copy in outs:
        copy.start()

    total = jnp.zeros((1, own_tokens), F32)
    grads = jnp.zeros((own_tokens, width), F32)
    for c in BLOCK_ORDER:
        b = block_of(c)
        for j in range(per):
            if c or j:
                s = partner(c, j)
                arrived(br.at[slot_rows(s)], s, b_r)
                arrived(pr.at[s], s, p_r)
        here = place(b).astype(F32)
        grads = grads + tn(here.astype(BF16), br[block_rows(b), :])
        line = pr[pl.ds(b * per, per)][:, 0:1, :]
        column = jnp.sum(jnp.where(diagonal, line, 0.0), axis=2, keepdims=True)
        total = total + jnp.sum(here * column.reshape(rows, 1), axis=0, keepdims=True)
    gt_out[...] = grads.astype(BF16)
    gp_out[...] = (total / prob_row).astype(BF16)

    for c in BLOCK_ORDER:
        for j in range(per):
            if c or j:
                for make in (out_tok, out_cot, back_grad, back_prob):
                    make(c, j).wait_send()
        for j in range(1, ndp):
            forward(rt, block_of(c), j, ft_s, ft_r).wait_send()
            forward(rs, block_of(c), j, fs_s, fs_r).wait_send()
    for copy in outs:
        copy.wait()


def hand_on(*refs):
    for src, dst in zip(refs[: len(refs) // 2], refs[len(refs) // 2 :]):
        dst[...] = src[...]


def handed_on(*arrays):
    steps = 4
    blocks = [
        pl.BlockSpec((a.shape[0] // steps, a.shape[1]), lambda i: (i, 0)) for a in arrays
    ]
    return pl.pallas_call(
        hand_on,
        grid=(steps,),
        out_shape=tuple(jax.ShapeDtypeStruct(a.shape, a.dtype) for a in arrays),
        in_specs=blocks,
        out_specs=tuple(blocks),
        compiler_params=pltpu.CompilerParams(vmem_limit_bytes=62 * 2**20),
    )(*arrays)


def local(n, ndp, tokens, cotangent, prob, assign, w_gate, w_up, w_down):
    own_tokens, width = tokens.shape
    ff = w_gate.shape[2]
    cap = -(-(3 * own_tokens // n) // 16) * 16
    slots = n * cap
    vmem, anywhere = pl.BlockSpec(memory_space=pltpu.VMEM), pl.BlockSpec(memory_space=pl.ANY)
    dma = pltpu.SemaphoreType.DMA
    shape = jax.ShapeDtypeStruct
    grad_tokens, grad_prob, grad_gate, grad_up, grad_down = pl.pallas_call(
        functools.partial(kernel, n, ndp, cap),
        out_shape=(
            shape((own_tokens, width), BF16),
            shape((1, own_tokens), BF16),
            shape((width // ndp, ff), F32),
            shape((width // ndp, ff), F32),
            shape((ff // ndp, width), F32),
        ),
        in_specs=[vmem] * 4 + [anywhere] * 3,
        out_specs=(vmem, vmem, anywhere, anywhere, anywhere),
        scratch_shapes=[
            pltpu.VMEM((width, ff), BF16),
            pltpu.VMEM((width, ff), BF16),
            pltpu.VMEM((ff, width), BF16),
            pltpu.VMEM((slots, width), BF16),
            pltpu.VMEM((slots, width), BF16),
            pltpu.VMEM((ndp, slots, width), BF16),
            pltpu.VMEM((ndp, slots, width), BF16),
            pltpu.VMEM((slots // BLOCKS, ff), BF16),
            pltpu.VMEM((slots // BLOCKS, ff), BF16),
            pltpu.VMEM((slots // BLOCKS, ff), BF16),
            pltpu.VMEM((3, width // ndp, ff), F32),
            pltpu.VMEM((slots, width), BF16),
            pltpu.VMEM((slots, width), BF16),
            pltpu.VMEM((n, 8, 128), F32),
            pltpu.VMEM((n, 8, 128), F32),
            dma((3,)),
            dma((n,)), dma((n,)), dma((n,)), dma((n,)),
            dma((ndp * BLOCKS,)), dma((ndp * BLOCKS,)),
            dma((ndp * BLOCKS,)), dma((ndp * BLOCKS,)),
            dma((n,)), dma((n,)), dma((n,)), dma((n,)),
            dma((3,)),
        ],
        compiler_params=pltpu.CompilerParams(
            collective_id=0, has_side_effects=True, vmem_limit_bytes=62 * 2**20
        ),
        cost_estimate=pl.CostEstimate(
            flops=22 * slots * width * ff, bytes_accessed=16 * width * ff, transcendentals=0
        ),
    )(
        tokens, cotangent, prob, assign.reshape(1, own_tokens),
        w_gate[0], w_up[0], w_down[0],
    )
    grad_tokens, grad_gate, grad_up, grad_down = handed_on(
        grad_tokens, grad_gate, grad_up, grad_down
    )
    return (
        grad_tokens, grad_prob.reshape(own_tokens),
        grad_gate[None], grad_up[None], grad_down[None],
    )


def solution(mesh):
    placed = (
        P(("dp", "expert"), None),
        P(("dp", "expert"), None),
        P(("dp", "expert")),
        P(("dp", "expert"), None),
        P("expert", None, None),
        P("expert", None, None),
        P("expert", None, None),
    )
    return jax.shard_map(
        functools.partial(local, mesh.shape["expert"], mesh.shape["dp"]),
        mesh=mesh,
        in_specs=placed,
        out_specs=(
            P(("dp", "expert"), None),
            P(("dp", "expert")),
            P("expert", "dp", None),
            P("expert", "dp", None),
            P("expert", "dp", None),
        ),
        check_vma=False,
    )
```

```python
import functools
import math

import jax
import jax.numpy as jnp
from jax import lax
from jax.experimental import pallas as pl
from jax.experimental.pallas import tpu as pltpu
from jax.sharding import PartitionSpec as P

MESH = pl.DeviceIdType.MESH
F32 = jnp.float32
BF16 = jnp.bfloat16
BLOCK_ORDER = (0, 2, 1, 3)
BLOCKS = 4


def tn(a, b):
    return lax.dot_general(a, b, (((0,), (0,)), ((), ())), preferred_element_type=F32)


def nt(a, b):
    return lax.dot_general(a, b, (((1,), (1,)), ((), ())), preferred_element_type=F32)


def nn(a, b):
    return jnp.dot(a, b, preferred_element_type=F32)


def kernel(
    n, ndp, cap,
    tok, cot, prob, assign, wg_hbm, wu_hbm, wd_hbm,
    gt_out, gp_out, gg_out, gu_out, gd_out,
    wg, wu, wd, st, ss, rt, rs, hid, ggp, gup, acc, acc16, mine, bs, br, ps, pr,
    w_sem, st_s, st_r, ss_s, ss_r, ft_s, ft_r, fs_s, fs_r, b_s, b_r, p_s, p_r, o_sem,
):
    k = lax.axis_index("dp")
    me = lax.axis_index("expert")
    own_tokens, width = tok.shape
    ff = wg.shape[1]
    per = n // BLOCKS
    rows = per * cap
    half = acc.shape[1]
    my_block, my_place = me // per, lax.rem(me, per)

    def block_of(c):
        high = lax.rem(my_block // 2 + c // 2, 2)
        low = lax.rem(lax.rem(my_block, 2) + c % 2, 2)
        return high * 2 + low

    def partner(c, j):
        return block_of(c) * per + lax.rem(my_place + j, per)

    def slot_rows(s):
        return pl.ds(pl.multiple_of(s * cap, 16), cap)

    def block_rows(b):
        return pl.ds(pl.multiple_of(b * rows, 16), rows)

    barrier = pltpu.get_barrier_semaphore()
    for c in range(BLOCKS):
        for j in range(per):
            if c or j:
                pl.semaphore_signal(
                    barrier, inc=1, device_id=(k, partner(c, j)), device_id_type=MESH
                )
    for j in range(1, ndp):
        pl.semaphore_signal(
            barrier, inc=1, device_id=(lax.rem(k + j, ndp), me), device_id_type=MESH
        )

    weights = [
        pltpu.make_async_copy(src, dst, w_sem.at[i])
        for i, (src, dst) in enumerate(((wg_hbm, wg), (wu_hbm, wu), (wd_hbm, wd)))
    ]
    for copy in weights:
        copy.start()

    expert = lax.broadcasted_iota(jnp.int32, (n, own_tokens), 0)
    chosen = (expert == assign[...]).astype(F32)
    earlier = (
        lax.broadcasted_iota(jnp.int32, (own_tokens, own_tokens), 0)
        < lax.broadcasted_iota(jnp.int32, (own_tokens, own_tokens), 1)
    ).astype(F32)
    before = nn(chosen.astype(BF16), earlier.astype(BF16))
    slot = jnp.sum(chosen * (before + expert.astype(F32) * cap), axis=0, keepdims=True)
    slot = slot.astype(jnp.int32)
    prob_row = prob[...].astype(F32).reshape(1, own_tokens)

    def place(b):
        return lax.broadcasted_iota(jnp.int32, (rows, own_tokens), 0) + b * rows == slot

    def to_slot(src, dst, s, send, recv, c, j):
        return pltpu.make_async_remote_copy(
            src_ref=src,
            dst_ref=dst,
            send_sem=send.at[c * per + j],
            recv_sem=recv.at[me],
            device_id=(k, s),
            device_id_type=MESH,
        )

    def out_tok(c, j):
        s = partner(c, j)
        return to_slot(st.at[slot_rows(s)], rt.at[k, slot_rows(me)], s, st_s, st_r, c, j)

    def out_cot(c, j):
        s = partner(c, j)
        return to_slot(ss.at[slot_rows(s)], rs.at[k, slot_rows(me)], s, ss_s, ss_r, c, j)

    def back_grad(c, j):
        s = partner(c, j)
        return to_slot(bs.at[slot_rows(s)], br.at[slot_rows(me)], s, b_s, b_r, c, j)

    def back_prob(c, j):
        s = partner(c, j)
        return to_slot(ps.at[s], pr.at[me], s, p_s, p_r, c, j)

    def arrived(buf, s, recv):
        pltpu.make_async_remote_copy(
            src_ref=buf, dst_ref=buf, send_sem=st_s.at[0], recv_sem=recv.at[s],
            device_id=(k, s), device_id_type=MESH,
        ).wait_recv()

    for step, c in enumerate(BLOCK_ORDER):
        b = block_of(c)
        here = place(b)
        st[block_rows(b), :] = nn(here.astype(F32).astype(BF16), tok[...]).astype(BF16)
        if step == 0:
            pl.semaphore_wait(barrier, n - 1 + ndp - 1)
        for j in range(per):
            if c or j:
                out_tok(c, j).start()
        ss[block_rows(b), :] = nn(
            jnp.where(here, prob_row, 0.0).astype(BF16), cot[...]
        ).astype(BF16)
        for j in range(per):
            if c or j:
                out_cot(c, j).start()
    rt[k, slot_rows(me), :] = st[slot_rows(me), :]
    rs[k, slot_rows(me), :] = ss[slot_rows(me), :]

    def forward(buf, b, j, send, recv):
        view = buf.at[k, block_rows(b)]
        return pltpu.make_async_remote_copy(
            src_ref=view,
            dst_ref=view,
            send_sem=send.at[(j - 1) * BLOCKS + b],
            recv_sem=recv.at[k * BLOCKS + b],
            device_id=(lax.rem(k + j, ndp), me),
            device_id_type=MESH,
        )

    tile = min(512, ff)

    def hidden_grads(g, b):
        here = block_rows(b)

        def body(i, total):
            cols = pl.ds(pl.multiple_of(i * tile, tile), tile)
            x = rt[g, here, :]
            gate = nn(x, wg[:, cols])
            up = nn(x, wu[:, cols])
            grad = nt(rs[g, here, :], wd[cols, :])
            s = jax.nn.sigmoid(gate)
            act = gate * s
            h = (act * up).astype(BF16)
            hid[:, cols] = h
            ggp[:, cols] = (grad * up * s * (1.0 + gate * (1.0 - s))).astype(BF16)
            gup[:, cols] = (grad * act).astype(BF16)
            return total + jnp.sum(grad * h.astype(F32), axis=1, keepdims=True)

        return lax.fori_loop(0, ff // tile, body, jnp.zeros((rows, 1), F32))

    diagonal = lax.broadcasted_iota(jnp.int32, (per, cap, 128), 1) == lax.broadcasted_iota(
        jnp.int32, (per, cap, 128), 2
    )

    def own_block(c):
        b = block_of(c)
        here = block_rows(b)
        dots = hidden_grads(k, b)

        def body(i, carry):
            cols = pl.ds(pl.multiple_of(i * tile, tile), tile)
            grad = nt(ggp[...], wg[cols, :]) + nt(gup[...], wu[cols, :])
            bs[here, cols] = grad.astype(BF16)
            return carry

        lax.fori_loop(0, width // tile, body, 0)
        line = jnp.sum(jnp.where(diagonal, dots.reshape(per, cap, 1), 0.0), axis=1, keepdims=True)
        ps[pl.ds(b * per, per)] = jnp.broadcast_to(line, (per, 8, 128))
        for j in range(per):
            if c or j:
                back_grad(c, j).start()
                back_prob(c, j).start()
        if c == 0:
            br[slot_rows(me), :] = bs[slot_rows(me), :]
            pr[me] = ps[me]

    mt = math.gcd(256, half)

    def weight_grads(g, b, first):
        here = block_rows(b)

        def body(i, carry):
            out = pl.ds(pl.multiple_of(i * mt, mt), mt)
            src = pl.ds(pl.multiple_of(k * half + i * mt, mt), mt)
            x = rt[g, here, src]
            terms = (tn(x, ggp[...]), tn(x, gup[...]), tn(hid[:, src], rs[g, here, :]))
            for m in range(3):
                if first:
                    acc[m, out, :] = terms[m]
                else:
                    acc[m, out, :] += terms[m]
            return carry

        lax.fori_loop(0, half // mt, body, 0)

    def peers_block(c):
        b = block_of(c)

        def body(j, carry):
            g = lax.rem(k + j, ndp)
            for buf, recv in ((rt, ft_r), (rs, fs_r)):
                view = buf.at[g, block_rows(b)]
                pltpu.make_async_remote_copy(
                    src_ref=view, dst_ref=view, send_sem=ft_s.at[0],
                    recv_sem=recv.at[g * BLOCKS + b],
                    device_id=(g, me), device_id_type=MESH,
                ).wait_recv()
            hidden_grads(g, b)
            weight_grads(g, b, False)
            return carry

        lax.fori_loop(1, ndp, body, 0)

    def in_order(c, first):
        b = block_of(c)
        for j in range(per):
            if c or j:
                s = partner(c, j)
                arrived(br.at[slot_rows(s)], s, b_r)
                arrived(pr.at[s], s, p_r)
        here = place(b).astype(F32)
        grads = tn(here.astype(BF16), br[block_rows(b), :])
        if first:
            mine[...] = grads
        else:
            mine[...] += grads
        line = pr[pl.ds(b * per, per)][:, 0:1, :]
        column = jnp.sum(jnp.where(diagonal, line, 0.0), axis=2, keepdims=True)
        return jnp.sum(here * column.reshape(rows, 1), axis=0, keepdims=True)

    for step, c in enumerate(BLOCK_ORDER):
        b = block_of(c)
        for j in range(per):
            if c or j:
                s = partner(c, j)
                arrived(rt.at[k, slot_rows(s)], s, st_r)
        for j in range(1, ndp):
            forward(rt, b, j, ft_s, ft_r).start()
        for j in range(per):
            if c or j:
                s = partner(c, j)
                arrived(rs.at[k, slot_rows(s)], s, ss_r)
        for j in range(1, ndp):
            forward(rs, b, j, fs_s, fs_r).start()
        if step == 0:
            for copy in weights:
                copy.wait()
        own_block(c)
        weight_grads(k, b, step == 0)
        if step:
            peers_block(BLOCK_ORDER[step - 1])
    total = in_order(BLOCK_ORDER[0], True)
    for c in BLOCK_ORDER[1:-1]:
        total = total + in_order(c, False)
    peers_block(BLOCK_ORDER[-1])
    outs = []
    for m, dst in enumerate((gg_out, gu_out, gd_out)):
        acc16[m] = acc[m].astype(BF16)
        outs.append(pltpu.make_async_copy(acc16.at[m], dst, o_sem.at[m]))
        outs[m].start()

    total = total + in_order(BLOCK_ORDER[-1], False)
    gt_out[...] = mine[...].astype(BF16)
    gp_out[...] = (total / prob_row).astype(BF16)

    for c in BLOCK_ORDER:
        for j in range(per):
            if c or j:
                for make in (out_tok, out_cot, back_grad, back_prob):
                    make(c, j).wait_send()
        for j in range(1, ndp):
            forward(rt, block_of(c), j, ft_s, ft_r).wait_send()
            forward(rs, block_of(c), j, fs_s, fs_r).wait_send()
    for copy in outs:
        copy.wait()


def hand_on(*refs):
    for src, dst in zip(refs[: len(refs) // 2], refs[len(refs) // 2 :]):
        dst[...] = src[...].astype(dst.dtype)


def handed_on(arrays, types):
    steps = 8
    blocks = [
        pl.BlockSpec((a.shape[0] // steps, a.shape[1]), lambda i: (i, 0)) for a in arrays
    ]
    return pl.pallas_call(
        hand_on,
        grid=(steps,),
        out_shape=tuple(jax.ShapeDtypeStruct(a.shape, t) for a, t in zip(arrays, types)),
        in_specs=blocks,
        out_specs=tuple(blocks),
        compiler_params=pltpu.CompilerParams(vmem_limit_bytes=62 * 2**20),
    )(*arrays)


def local(n, ndp, tokens, cotangent, prob, assign, w_gate, w_up, w_down):
    own_tokens, width = tokens.shape
    ff = w_gate.shape[2]
    cap = -(-(3 * own_tokens // n) // 16) * 16
    slots = n * cap
    vmem, anywhere = pl.BlockSpec(memory_space=pltpu.VMEM), pl.BlockSpec(memory_space=pl.ANY)
    dma = pltpu.SemaphoreType.DMA
    shape = jax.ShapeDtypeStruct
    grad_tokens, grad_prob, grad_gate, grad_up, grad_down = pl.pallas_call(
        functools.partial(kernel, n, ndp, cap),
        out_shape=(
            shape((own_tokens, width), BF16),
            shape((1, own_tokens), BF16),
            shape((width // ndp, ff), BF16),
            shape((width // ndp, ff), BF16),
            shape((ff // ndp, width), BF16),
        ),
        in_specs=[vmem] * 4 + [anywhere] * 3,
        out_specs=(vmem, vmem, anywhere, anywhere, anywhere),
        scratch_shapes=[
            pltpu.VMEM((width, ff), BF16),
            pltpu.VMEM((width, ff), BF16),
            pltpu.VMEM((ff, width), BF16),
            pltpu.VMEM((slots, width), BF16),
            pltpu.VMEM((slots, width), BF16),
            pltpu.VMEM((ndp, slots, width), BF16),
            pltpu.VMEM((ndp, slots, width), BF16),
            pltpu.VMEM((slots // BLOCKS, ff), BF16),
            pltpu.VMEM((slots // BLOCKS, ff), BF16),
            pltpu.VMEM((slots // BLOCKS, ff), BF16),
            pltpu.VMEM((3, width // ndp, ff), F32),
            pltpu.VMEM((3, width // ndp, ff), BF16),
            pltpu.VMEM((own_tokens, width), F32),
            pltpu.VMEM((slots, width), BF16),
            pltpu.VMEM((slots, width), BF16),
            pltpu.VMEM((n, 8, 128), F32),
            pltpu.VMEM((n, 8, 128), F32),
            dma((3,)),
            dma((n,)), dma((n,)), dma((n,)), dma((n,)),
            dma((ndp * BLOCKS,)), dma((ndp * BLOCKS,)),
            dma((ndp * BLOCKS,)), dma((ndp * BLOCKS,)),
            dma((n,)), dma((n,)), dma((n,)), dma((n,)),
            dma((3,)),
        ],
        compiler_params=pltpu.CompilerParams(
            collective_id=0, has_side_effects=True, vmem_limit_bytes=62 * 2**20
        ),
        cost_estimate=pl.CostEstimate(
            flops=22 * slots * width * ff, bytes_accessed=16 * width * ff, transcendentals=0
        ),
    )(
        tokens, cotangent, prob, assign.reshape(1, own_tokens),
        w_gate[0], w_up[0], w_down[0],
    )
    grad_tokens, grad_gate, grad_up, grad_down = handed_on(
        (grad_tokens, grad_gate, grad_up, grad_down), (BF16, F32, F32, F32)
    )
    return (
        grad_tokens, grad_prob.reshape(own_tokens),
        grad_gate[None], grad_up[None], grad_down[None],
    )


def solution(mesh):
    placed = (
        P(("dp", "expert"), None),
        P(("dp", "expert"), None),
        P(("dp", "expert")),
        P(("dp", "expert"), None),
        P("expert", None, None),
        P("expert", None, None),
        P("expert", None, None),
    )
    return jax.shard_map(
        functools.partial(local, mesh.shape["expert"], mesh.shape["dp"]),
        mesh=mesh,
        in_specs=placed,
        out_specs=(
            P(("dp", "expert"), None),
            P(("dp", "expert")),
            P("expert", "dp", None),
            P("expert", "dp", None),
            P("expert", "dp", None),
        ),
        check_vma=False,
    )
```
